256 devices in a mesh: op: 64 (over z, x, core), sec: 4 (over y).
Axes of the slice: x: 4, y: 4, z: 8, core: 2. Of those that a mesh axis runs over, the one named last changes fastest.
Arguments:
- wavefunction: bfloat16 [40, 128, 128], P('sec'), may hold values from -6 to 6
- diagonal: float32 [40, 128, 128], P('sec'), may hold values from -2 to 2
- left_ops: bfloat16 [1024, 40, 128, 128], P('op', 'sec'), may hold values from -0.15 to 0.2171875
- right_ops: bfloat16 [1024, 40, 128, 128], P('op', 'sec'), may hold values from -0.6 to 1.6
- connect: int32 [1024, 40], P('op', 'sec'), may hold values from 0 to 40, as said below
Outputs:
- sigma_one: bfloat16 [40, 128, 128], P('sec')
- correction: bfloat16 [40, 128, 128], P('sec')
- sigma_two: bfloat16 [40, 128, 128], P('sec')
The draws below stay inside these ranges and needn't reach their ends.
Inputs may be any that keep to these rules, and one draw needn't show every extreme that they name: connect[p,b] is (b + s_p) mod 40 for a shift s_p of pair p, or 40 where pair p does not act into sector b.
All inputs are finite; a program needn't handle non-finite values.
Results may differ from the reference program's by a relative error of at most 0.005.
Values may be sent and summed in bfloat16 or wider, within the bound.
A program may use at most 128 MiB of HBM per device.

```python
import jax
import jax.numpy as jnp
from jax import lax

BS = 128
PAIRS = 1024
NSEC = 40


def draw_connect(key, part):
    key = jax.random.fold_in(key, 7)
    key_shift, key_level, key_roll = jax.random.split(key, 3)
    pair_ids = jnp.arange(PAIRS, dtype=jnp.int32)[:, None]
    targets = jnp.arange(NSEC, dtype=jnp.int32)[None, :]
    shifts = jax.random.randint(key_shift, (PAIRS, 1), 0, NSEC, dtype=jnp.int32)
    shifts = jnp.where(pair_ids == 0, NSEC - 1, shifts)
    levels = jax.random.randint(key_level, (PAIRS, 1), 1, 5, dtype=jnp.int32)
    levels = jnp.where(pair_ids == 0, 4, levels)
    rolls = jax.random.randint(key_roll, (PAIRS, NSEC), 0, 4, dtype=jnp.int32)
    sources = (targets + shifts) % NSEC
    forced = (pair_ids == 0) & (targets == 0)
    live = (rolls < levels) & jnp.logical_not(forced)
    return jnp.where(live, sources, NSEC).astype(jnp.int32)


def draw_left_ops(key, part):
    key = jax.random.fold_in(key, 11)
    shape = (PAIRS, NSEC, BS, BS)
    sector_pos = jnp.arange(NSEC, dtype=jnp.float32)[None, :, None, None] / (NSEC - 1)
    identity = jnp.eye(BS, dtype=jnp.float32)[None, None, :, :]
    noise = jax.random.truncated_normal(key, -6.0, 6.0, shape, jnp.float32)
    gains = 0.5 * jnp.power(3.0, sector_pos)
    scale_noise = 1.0 / jnp.sqrt(jnp.float32(BS * PAIRS))
    values = noise * scale_noise + identity * gains * (NSEC / PAIRS)
    return values.astype(jnp.bfloat16)


def draw_right_ops(key, part):
    key = jax.random.fold_in(key, 13)
    shape = (PAIRS, NSEC, BS, BS)
    identity = jnp.eye(BS, dtype=jnp.float32)[None, None, :, :]
    noise = jax.random.truncated_normal(key, -6.0, 6.0, shape, jnp.float32)
    values = identity + noise / jnp.sqrt(jnp.float32(BS))
    return values.astype(jnp.bfloat16)


def level_of(own_key, shape, cuts, smallest, top_value):
    factor_of, own = 1.0, jax.random.fold_in(own_key, 6)
    for axis_at, parts in cuts:
        heights = jnp.exp(jax.random.uniform(jax.random.fold_in(own, axis_at), (parts,), jnp.float32, smallest / len(cuts), top_value / len(cuts)))
        factor_of = factor_of * jnp.repeat(heights, shape[axis_at] // parts).reshape([-1 if axis == axis_at else 1 for axis in range(len(shape))])
    return factor_of


def bell_draw(key, shape, deviation, reach, cuts=(), kind=jnp.bfloat16):
    drawn = jax.random.normal(key, shape, jnp.float32) * deviation
    if len(cuts) > 0:
        drawn = level_of(key, shape, cuts, -0.22, 0.18) * drawn
    return jnp.clip(drawn, min=-reach, max=reach).astype(kind)


def setup_inputs(seed: int = 0) -> dict:
    seeds = jax.random.split(jax.random.key(seed), 6)
    wavefunction = bell_draw(seeds[0], (NSEC, BS, BS), 1.0, 6.0, ((0, 4),))
    diagonal = jnp.clip(jax.random.uniform(seeds[1], (NSEC, BS, BS), jnp.float32, -2.0, 2.0) * level_of(seeds[1], (NSEC, BS, BS), ((0, 4),), -0.4, 0.0), -2.0, 2.0)
    left_ops = draw_left_ops(jax.random.fold_in(seeds[5], 71), 0)
    right_ops = draw_right_ops(jax.random.fold_in(seeds[5], 71), 0)
    connect = draw_connect(jax.random.fold_in(seeds[5], 71), 0)
    return dict(wavefunction=wavefunction, diagonal=diagonal, left_ops=left_ops, right_ops=right_ops, connect=connect)


def apply_pairs(vector, left_ops, right_ops, connect):
    padded = jnp.concatenate([vector, jnp.zeros((1, BS, BS), vector.dtype)], axis=0)

    def add_pair(total, items):
        left_one, right_one, links = items
        sources = padded[links.astype(jnp.int32)]
        halfway = jnp.einsum('sij,sjk->sik', left_one.astype(jnp.float32), sources.astype(jnp.float32)).astype(jnp.bfloat16)
        products = jnp.einsum('sik,slk->sil', halfway.astype(jnp.float32), right_one.astype(jnp.float32))
        return (total + products, None)
    start = jnp.zeros((NSEC, BS, BS), jnp.float32)
    total, unused = lax.scan(add_pair, start, (left_ops, right_ops, connect))
    return total

def reference(wavefunction, diagonal, left_ops, right_ops, connect):
    sigma = apply_pairs(wavefunction, left_ops, right_ops, connect)
    psi_wide = wavefunction.astype(jnp.float32)
    correlation = jnp.sum(psi_wide * sigma)
    weight = jnp.sum(psi_wide * psi_wide)
    rayleigh = correlation / weight
    shifted = diagonal - rayleigh
    unscaled = (sigma - rayleigh * psi_wide) * shifted / (shifted * shifted + 1.0)
    along = jnp.sum(psi_wide * unscaled)
    squares = jnp.sum(unscaled * unscaled)
    rescale = 1.0 / jnp.sqrt((squares - along * along / weight) / (NSEC * BS * BS) + 1e-06)
    correction = ((unscaled - along / weight * psi_wide) * rescale).astype(jnp.bfloat16)
    sigma_two = apply_pairs(correction, left_ops, right_ops, connect)
    return (sigma.astype(jnp.bfloat16), correction, sigma_two.astype(jnp.bfloat16))
```

```python
import functools

import jax
import jax.numpy as jnp
from jax import lax
from jax.experimental import pallas as pl
from jax.experimental.pallas import tpu as pltpu
from jax.sharding import PartitionSpec as P

MESH = pl.DeviceIdType.MESH
BS = 128
NZ, NX, NC, NY = 8, 4, 2, 4
PLANE = NZ * NX * NC
SECD = 10
HALF = SECD // NC
PIECE = BS // NX
NSEC = SECD * NY
PAIRD = 16
NT = (((1,), (1,)), ((), ()))
FAR_Z = (4, 3, 5, 2, 6, 1, 7)
FAR_Y = (2, 1, 3)
FAR_X = (2, 1, 3)
LOADS = 4


def sum_z(k):
    return (NZ * k) // HALF


def kernel(
    psi_hbm, diag_hbm, left_hbm, right_hbm, link,
    one_out, corr_out, two_out,
    left, right, vec, diag, sig, raw, corr, part, inbox, two,
    load_sem, out_sem, vsend, vrecv, vfsend, vfrecv, dsend, drecv, dfsend, dfrecv,
    rs_send, rs_recv, z_send, z_recv, xy_send, xy_recv, sib_send, sib_recv,
    x_send, x_recv, sib2_send, sib2_recv,
):
    op = lax.axis_index("op")
    y = lax.axis_index("sec")
    z, x, c = op // (NX * NC), (op // NC) % NX, op % NC

    def at(z_, x_, c_, y_):
        return ((z_ * NX + x_) * NC + c_, y_)

    sibling = at(z, x, 1 - c, y)

    def remote(src, dst, send, recv, device):
        return pltpu.make_async_remote_copy(
            src_ref=src, dst_ref=dst, send_sem=send, recv_sem=recv, device_id=device, device_id_type=MESH
        )

    def settle(ref, sem):
        pltpu.make_async_copy(ref, ref, sem).wait()

    per = PAIRD // LOADS
    loads = []
    for n in range(LOADS):
        rows = pl.ds(n * per, per)
        loads.append(pltpu.make_async_copy(left_hbm.at[rows], left.at[rows], load_sem.at[2 * n]))
        loads.append(pltpu.make_async_copy(right_hbm.at[rows], right.at[rows], load_sem.at[2 * n + 1]))
    own_vec = pltpu.make_async_copy(psi_hbm, vec.at[pl.ds(y * SECD, SECD)], load_sem.at[2 * LOADS])
    own_diag = pltpu.make_async_copy(diag_hbm, diag.at[pl.ds(y * SECD, SECD)], load_sem.at[2 * LOADS + 1])
    own_vec.start()
    for load in loads:
        load.start()
    own_diag.start()

    barrier = pltpu.get_barrier_semaphore()

    def greet(i, _):
        pl.semaphore_signal(barrier, inc=1, device_id=((op + i) % PLANE, y), device_id_type=MESH)
        return 0

    for dy in FAR_Y:
        for dx in range(NX):
            pl.semaphore_signal(
                barrier, inc=1, device_id=at(z, (x + dx) % NX, c, (y + dy) % NY), device_id_type=MESH
            )
    lax.fori_loop(1, PLANE, greet, 0)
    vec[NSEC] = jnp.zeros((BS, BS), jnp.bfloat16)
    corr[NSEC] = jnp.zeros((BS, BS), jnp.bfloat16)
    pl.semaphore_wait(barrier, PLANE - 1 + (NY - 1) * NX)

    for dy in FAR_Y:
        there = at(z, x, c, (y + dy) % NY)
        remote(
            psi_hbm.at[pl.ds(c * HALF, HALF)], vec.at[pl.ds(y * SECD + c * HALF, HALF)],
            vsend, vrecv.at[dy], there,
        ).start()
    own_vec.wait()
    for dy in (1, 3, 2):
        rows = pl.ds(((y + NY - dy) % NY) * SECD + c * HALF, HALF)
        settle(vec.at[rows], vrecv.at[dy])
        remote(vec.at[rows], vec.at[rows], vfsend, vfrecv.at[dy], sibling).start()
    for dy in FAR_Y:
        there = at(z, x, c, (y + dy) % NY)
        remote(
            diag_hbm.at[pl.ds(c * HALF, HALF)], diag.at[pl.ds(y * SECD + c * HALF, HALF)],
            dsend, drecv.at[dy], there,
        ).start()
    for load in loads:
        load.wait()
    for dy in (1, 3, 2):
        rows = pl.ds(((y + NY - dy) % NY) * SECD + (1 - c) * HALF, HALF)
        settle(vec.at[rows], vfrecv.at[dy])

    k_me = (HALF * z + HALF + 2) // NZ
    summing = sum_z(k_me) == z
    mine = pl.ds(x * PIECE, PIECE)

    def apply(which, vector):
        def sector(i, _):
            core, k = i % NC, i // NC
            b = core * HALF + k
            halves = []
            for p in range(PAIRD):
                half = jnp.dot(left[p, b], vector[link[p, b]], preferred_element_type=jnp.float32)
                halves.append(half.astype(jnp.bfloat16))
            halfway = jnp.concatenate(halves, axis=1)
            wide = jnp.concatenate([right[p, b] for p in range(PAIRD)], axis=1)
            total = lax.dot_general(halfway, wide, NT, preferred_element_type=jnp.float32)
            part[which, b] = total.astype(jnp.bfloat16)

            def piece(j, _):
                rows = pl.ds(j * PIECE, PIECE)
                owner = (sum_z(k) * NX + j) * NC + core

                @pl.when(owner == op)
                def _():
                    inbox[which, op] = part[which, b, rows]

                @pl.when(owner != op)
                def _():
                    remote(
                        part.at[which, b, rows], inbox.at[which, op],
                        rs_send.at[which], rs_recv.at[which], (owner, y),
                    ).start()

                return 0

            lax.fori_loop(0, NX, piece, 0)
            return 0

        lax.fori_loop(0, SECD, sector, 0)

    def summed(which):
        settle(inbox.at[which, pl.ds(0, PLANE - 1)], rs_recv.at[which])
        return jnp.sum(inbox[which].astype(jnp.float32), axis=0).astype(jnp.bfloat16)

    apply(0, vec)

    @pl.when(summing)
    def _():
        spot = sig.at[y, c * HALF + k_me, mine]
        spot[...] = summed(0)
        for dz in FAR_Z:
            remote(spot, spot, z_send.at[0], z_recv.at[0, k_me], at((z + dz) % NZ, x, c, y)).start()

    def spread(k, _):
        spot = sig.at[y, c * HALF + k, mine]

        @pl.when(sum_z(k) != z)
        def _():
            settle(spot, z_recv.at[0, k])

        for dy in (2, 1, 3, 0):
            for dx in (2, 1, 3, 0):
                if dx or dy:
                    there = at(z, (x + dx) % NX, c, (y + dy) % NY)
                    remote(spot, spot, xy_send.at[k], xy_recv.at[k], there).start()
        return 0

    lax.fori_loop(0, HALF, spread, 0)
    for dy in (1, 3, 2):
        rows = pl.ds(((y + NY - dy) % NY) * SECD + c * HALF, HALF)
        settle(diag.at[rows], drecv.at[dy])
        remote(diag.at[rows], diag.at[rows], dfsend, dfrecv.at[dy], sibling).start()

    def hand(k, _):
        settle(inbox.at[0, pl.ds(0, NX * NY - 1)], xy_recv.at[k])
        spot = sig.at[:, c * HALF + k]
        remote(spot, spot, sib_send, sib_recv.at[k], sibling).start()
        return 0

    lax.fori_loop(0, HALF, hand, 0)
    own_diag.wait()
    for dy in (1, 3, 2):
        rows = pl.ds(((y + NY - dy) % NY) * SECD + (1 - c) * HALF, HALF)
        settle(diag.at[rows], dfrecv.at[dy])
    for k in range(HALF):
        settle(sig.at[:, (1 - c) * HALF + k], sib_recv.at[k])
    one_copy = pltpu.make_async_copy(sig.at[y], one_out, out_sem.at[0])
    one_copy.start()

    def fold(block):
        return jnp.sum(block.reshape(BS // 8, 8, BS), axis=0)

    def first(s, sums):
        psi = vec[s].astype(jnp.float32)
        sigma = sig[s // SECD, s % SECD].astype(jnp.float32)
        return sums[0] + fold(psi * sigma), sums[1] + fold(psi * psi)

    zero = jnp.zeros((8, BS), jnp.float32)
    correlation, weight = lax.fori_loop(0, NSEC, first, (zero, zero))
    correlation = jnp.sum(correlation, keepdims=True)
    weight = jnp.sum(weight, keepdims=True)
    rayleigh = correlation / weight

    def second(s, sums):
        psi = vec[s].astype(jnp.float32)
        sigma = sig[s // SECD, s % SECD].astype(jnp.float32)
        shifted = diag[s] - rayleigh
        unscaled = (sigma - rayleigh * psi) * shifted / (shifted * shifted + 1.0)
        raw[s] = unscaled
        return sums[0] + fold(psi * unscaled), sums[1] + fold(unscaled * unscaled)

    along, squares = lax.fori_loop(0, NSEC, second, (zero, zero))
    along = jnp.sum(along, keepdims=True)
    squares = jnp.sum(squares, keepdims=True)
    rescale = 1.0 / jnp.sqrt((squares - along * along / weight) / float(NSEC * BS * BS) + 1e-06)
    share = along / weight

    def third(s, _):
        psi = vec[s].astype(jnp.float32)
        corr[s] = ((raw[s] - share * psi) * rescale).astype(jnp.bfloat16)
        return 0

    lax.fori_loop(0, NSEC, third, 0)
    corr_copy = pltpu.make_async_copy(corr.at[pl.ds(y * SECD, SECD)], corr_out, out_sem.at[1])
    corr_copy.start()

    apply(1, corr)

    @pl.when(summing)
    def _():
        spot = two.at[c * HALF + k_me, mine]
        spot[...] = summed(1)
        for dz in FAR_Z:
            remote(spot, spot, z_send.at[1], z_recv.at[1, k_me], at((z + dz) % NZ, x, c, y)).start()

    def spread_two(k, _):
        spot = two.at[c * HALF + k, mine]

        @pl.when(sum_z(k) != z)
        def _():
            settle(spot, z_recv.at[1, k])

        for dx in FAR_X:
            remote(spot, spot, x_send, x_recv.at[k], at(z, (x + dx) % NX, c, y)).start()
        return 0

    lax.fori_loop(0, HALF, spread_two, 0)

    def hand_two(k, _):
        settle(inbox.at[1, pl.ds(0, NX - 1)], x_recv.at[k])
        spot = two.at[c * HALF + k]
        remote(spot, spot, sib2_send, sib2_recv.at[k], sibling).start()
        return 0

    lax.fori_loop(0, HALF, hand_two, 0)
    for k in range(HALF):
        settle(two.at[(1 - c) * HALF + k], sib2_recv.at[k])
    two_copy = pltpu.make_async_copy(two, two_out, out_sem.at[2])
    two_copy.start()

    settle(vec.at[pl.ds(0, (NY - 1) * HALF)], vsend)
    settle(vec.at[pl.ds(0, (NY - 1) * HALF)], vfsend)
    settle(diag.at[pl.ds(0, (NY - 1) * HALF)], dsend)
    settle(diag.at[pl.ds(0, (NY - 1) * HALF)], dfsend)
    for which in range(2):

        @pl.when(summing)
        def _():
            settle(inbox.at[which, pl.ds(0, SECD * NX - 1)], rs_send.at[which])
            settle(inbox.at[which, pl.ds(0, NZ - 1)], z_send.at[which])

        @pl.when(jnp.logical_not(summing))
        def _():
            settle(inbox.at[which, pl.ds(0, SECD * NX)], rs_send.at[which])

    for k in range(HALF):
        settle(inbox.at[0, pl.ds(0, NX * NY - 1)], xy_send.at[k])
    settle(vec.at[pl.ds(0, NY * HALF)], sib_send)
    settle(inbox.at[0, pl.ds(0, HALF * (NX - 1))], x_send)
    settle(vec.at[pl.ds(0, HALF)], sib2_send)
    one_copy.wait()
    corr_copy.wait()
    two_copy.wait()


def per_device(wavefunction, diagonal, left_ops, right_ops, connect):
    blocks = jax.ShapeDtypeStruct((SECD, BS, BS), jnp.bfloat16)
    dma = pltpu.SemaphoreType.DMA
    hbm = pl.BlockSpec(memory_space=pl.ANY)
    return pl.pallas_call(
        kernel,
        out_shape=(blocks, blocks, blocks),
        in_specs=[hbm, hbm, hbm, hbm, pl.BlockSpec(memory_space=pltpu.SMEM)],
        out_specs=(hbm, hbm, hbm),
        scratch_shapes=[
            pltpu.VMEM((PAIRD, SECD, BS, BS), jnp.bfloat16),
            pltpu.VMEM((PAIRD, SECD, BS, BS), jnp.bfloat16),
            pltpu.VMEM((NSEC + 1, BS, BS), jnp.bfloat16),
            pltpu.VMEM((NSEC, BS, BS), jnp.float32),
            pltpu.VMEM((NY, SECD, BS, BS), jnp.bfloat16),
            pltpu.VMEM((NSEC, BS, BS), jnp.float32),
            pltpu.VMEM((NSEC + 1, BS, BS), jnp.bfloat16),
            pltpu.VMEM((2, SECD, BS, BS), jnp.bfloat16),
            pltpu.VMEM((2, PLANE, PIECE, BS), jnp.bfloat16),
            pltpu.VMEM((SECD, BS, BS), jnp.bfloat16),
            dma((2 * LOADS + 2,)), dma((3,)),
            dma, dma((NY,)), dma, dma((NY,)), dma, dma((NY,)), dma, dma((NY,)),
            dma((2,)), dma((2,)), dma((2,)), dma((2, HALF)),
            dma((HALF,)), dma((HALF,)), dma, dma((HALF,)),
            dma, dma((HALF,)), dma, dma((HALF,)),
        ],
        compiler_params=pltpu.CompilerParams(
            collective_id=0, has_side_effects=True, vmem_limit_bytes=40 * 2**20
        ),
        name="davidson",
    )(wavefunction, diagonal, left_ops, right_ops, connect)


def solution(mesh):
    blocks = P("sec", None, None)
    ops = P("op", "sec", None, None)
    return jax.shard_map(
        per_device,
        mesh=mesh,
        in_specs=(blocks, blocks, ops, ops, P("op", "sec")),
        out_specs=(blocks, blocks, blocks),
        check_vma=False,
    )
```

```python
import functools

import jax
import jax.numpy as jnp
from jax import lax
from jax.experimental import pallas as pl
from jax.experimental.pallas import tpu as pltpu
from jax.sharding import PartitionSpec as P

MESH = pl.DeviceIdType.MESH
BS = 128
NZ, NX, NC, NY = 8, 4, 2, 4
GROUP = NX * NC
SECD = 10
HALF = SECD // NC
PIECE = BS // NX
NSEC = SECD * NY
PAIRD = 16
NT = (((1,), (1,)), ((), ()))
FAR_Z = (4, 3, 5, 2, 6, 1, 7)
FAR = (2, 1, 3)
LOADS = 4


def reciprocal(q):
    guess = pl.reciprocal(q, approx=True)
    guess = guess * (2.0 - q * guess)
    return guess * (2.0 - q * guess)


def kernel(
    psi_hbm, diag_hbm, left_hbm, right_hbm, link,
    one_out, corr_out, two_out,
    left, right, vec, diag, sig, raw, corr, part, inbox, zbox, two,
    load_sem, out_sem, vsend, vrecv, vfsend, vfrecv, dsend, drecv, dfsend, dfrecv,
    s1_send, s1_recv, z_send, z_recv, xy_send, xy_recv, sib_send, sib_recv,
    x_send, x_recv,
):
    op = lax.axis_index("op")
    y = lax.axis_index("sec")
    z, x, c = op // (NX * NC), (op // NC) % NX, op % NC

    def at(z_, x_, c_, y_):
        return ((z_ * NX + x_) * NC + c_, y_)

    sibling = at(z, x, 1 - c, y)

    def send(src, dst, send_sem, recv_sem, device):
        pltpu.make_async_remote_copy(
            src_ref=src, dst_ref=dst, send_sem=send_sem, recv_sem=recv_sem, device_id=device, device_id_type=MESH
        ).start()

    def settle(ref, sem):
        pltpu.make_async_copy(ref, ref, sem).wait()

    per = PAIRD // LOADS
    loads = []
    for n in range(LOADS):
        rows = pl.ds(n * per, per)
        loads.append(pltpu.make_async_copy(left_hbm.at[rows], left.at[rows], load_sem.at[2 * n]))
        loads.append(pltpu.make_async_copy(right_hbm.at[rows], right.at[rows], load_sem.at[2 * n + 1]))
    own_vec = pltpu.make_async_copy(psi_hbm, vec.at[pl.ds(y * SECD, SECD)], load_sem.at[2 * LOADS])
    own_diag = pltpu.make_async_copy(diag_hbm, diag.at[pl.ds(y * SECD, SECD)], load_sem.at[2 * LOADS + 1])
    own_vec.start()
    for load in loads:
        load.start()
    own_diag.start()

    barrier = pltpu.get_barrier_semaphore()
    friends = [at((z + dz) % NZ, x, c, y) for dz in FAR_Z]
    friends += [at(z, (x + dx) % NX, c, (y + dy) % NY) for dy in FAR for dx in range(NX)]
    friends += [at(z, (x + dx) % NX, core, y) for dx in FAR for core in range(NC)]
    friends.append(sibling)
    for friend in friends:
        pl.semaphore_signal(barrier, inc=1, device_id=friend, device_id_type=MESH)
    vec[NSEC] = jnp.zeros((BS, BS), jnp.bfloat16)
    corr[NSEC] = jnp.zeros((BS, BS), jnp.bfloat16)
    pl.semaphore_wait(barrier, len(friends))

    up, down = at(z, x, c, (y + 1) % NY), at(z, x, c, (y + NY - 1) % NY)

    def spot_of(ref, dy, core, rows):
        return ref.at[pl.ds(((y + dy) % NY) * SECD + core * HALF, HALF), rows]

    halves_of = (pl.ds(0, BS // 2), pl.ds(BS // 2, BS // 2))
    whole = pl.ds(0, BS)

    def gather_start(src, dst, ssem, rsem):
        for n, (there, h) in enumerate(((up, 0), (down, 1), (up, 1), (down, 0))):
            send(
                src.at[pl.ds(c * HALF, HALF), halves_of[h]], spot_of(dst, 0, c, halves_of[h]),
                ssem, rsem.at[n], there,
            )

    def gather_forward(dst, ssem, rsem):
        for dy, there, h, n in ((NY - 1, up, 0, 0), (1, down, 1, 1)):
            spot = spot_of(dst, dy, c, halves_of[h])
            settle(spot, rsem.at[n])
            send(spot, spot, ssem, rsem.at[4 + n], there)

    def gather_share(dst, rsem, fssem, frsem):
        for dy, waits in ((NY - 1, (2,)), (1, (3,)), (2, (4, 5))):
            for n in waits:
                settle(spot_of(dst, dy, c, halves_of[0]), rsem.at[n])
            spot = spot_of(dst, dy, c, whole)
            send(spot, spot, fssem, frsem.at[dy], sibling)

    def gather_end(dst, frsem):
        for dy in (NY - 1, 1, 2):
            settle(spot_of(dst, dy, 1 - c, whole), frsem.at[dy])

    gather_start(psi_hbm, vec, vsend, vrecv)
    own_vec.wait()
    gather_forward(vec, vsend, vrecv)
    gather_share(vec, vrecv, vfsend, vfrecv)
    gather_start(diag_hbm, diag, dsend, drecv)
    for load in loads:
        load.wait()
    gather_end(vec, vfrecv)

    mine = pl.ds(x * PIECE, PIECE)

    def apply(which, vector):
        def sector(i, _):
            core, k = i % NC, i // NC
            b = core * HALF + k
            halves = []
            for p in range(PAIRD):
                half = jnp.dot(left[p, b], vector[link[p, b]], preferred_element_type=jnp.float32)
                halves.append(half.astype(jnp.bfloat16))
            halfway = jnp.concatenate(halves, axis=1)
            wide = jnp.concatenate([right[p, b] for p in range(PAIRD)], axis=1)
            total = lax.dot_general(halfway, wide, NT, preferred_element_type=jnp.float32)
            part[which, b] = total.astype(jnp.bfloat16)

            def piece(j, _):
                rows = pl.ds(j * PIECE, PIECE)
                own = jnp.logical_and(core == c, j == x)

                @pl.when(own)
                def _():
                    inbox[which, k, x * NC + c] = part[which, b, rows]

                @pl.when(jnp.logical_not(own))
                def _():
                    send(
                        part.at[which, b, rows], inbox.at[which, k, x * NC + c],
                        s1_send.at[which], s1_recv.at[which, k], at(z, j, core, y),
                    )

                return 0

            lax.fori_loop(0, NX, piece, 0)
            return 0

        lax.fori_loop(0, SECD, sector, 0)

    def added(box, which, k, count):
        total = box[which, k, 0].astype(jnp.float32)
        for n in range(1, count):
            total = total + box[which, k, n].astype(jnp.float32)
        return total.astype(jnp.bfloat16)

    def sum_near(which):
        def step(k, _):
            settle(inbox.at[which, k, pl.ds(0, GROUP - 1)], s1_recv.at[which, k])
            zbox[which, k, z] = added(inbox, which, k, GROUP)
            spot = zbox.at[which, k, z]
            for dz in FAR_Z:
                send(spot, spot, z_send.at[which], z_recv.at[which, k], at((z + dz) % NZ, x, c, y))
            return 0

        lax.fori_loop(0, HALF, step, 0)

    def sum_far(which, k):
        settle(zbox.at[which, k, pl.ds(0, NZ - 1)], z_recv.at[which, k])
        return added(zbox, which, k, NZ)

    apply(0, vec)
    gather_forward(diag, dsend, drecv)
    sum_near(0)
    gather_share(diag, drecv, dfsend, dfrecv)

    def spread(k, _):
        spot = sig.at[y, c * HALF + k, mine]
        spot[...] = sum_far(0, k)
        for dy in (2, 1, 3, 0):
            for dx in (2, 1, 3, 0):
                if dx or dy:
                    there = at(z, (x + dx) % NX, c, (y + dy) % NY)
                    send(spot, spot, xy_send.at[k], xy_recv.at[k], there)
        return 0

    lax.fori_loop(0, HALF, spread, 0)

    def fold(block):
        return jnp.sum(block.reshape(BS // 8, 8, BS), axis=0)

    def first(core, k, sums):
        for g in range(NY):
            psi = vec[g * SECD + core * HALF + k].astype(jnp.float32)
            sigma = sig[g, core * HALF + k].astype(jnp.float32)
            sums = sums[0] + fold(psi * sigma), sums[1] + fold(psi * psi)
        return sums

    def hand(k, sums):
        settle(inbox.at[0, pl.ds(0, 3), pl.ds(0, NX * NY // 3)], xy_recv.at[k])
        spot = sig.at[:, c * HALF + k]
        send(spot, spot, sib_send, sib_recv.at[k], sibling)
        return first(c, k, sums)

    def handed(k, sums):
        settle(sig.at[:, (1 - c) * HALF + k], sib_recv.at[k])
        return first(1 - c, k, sums)

    zero = jnp.zeros((8, BS), jnp.float32)
    sums = lax.fori_loop(0, HALF, hand, (zero, zero))
    correlation, weight = lax.fori_loop(0, HALF, handed, sums)
    one_copy = pltpu.make_async_copy(sig.at[y], one_out, out_sem.at[0])
    one_copy.start()
    own_diag.wait()
    gather_end(diag, dfrecv)

    correlation = jnp.sum(correlation, keepdims=True)
    weight = jnp.sum(weight, keepdims=True)
    rayleigh = correlation / weight

    def second(s, sums):
        psi = vec[s].astype(jnp.float32)
        sigma = sig[s // SECD, s % SECD].astype(jnp.float32)
        shifted = diag[s] - rayleigh
        unscaled = (sigma - rayleigh * psi) * shifted * reciprocal(shifted * shifted + 1.0)
        raw[s] = unscaled
        return sums[0] + fold(psi * unscaled), sums[1] + fold(unscaled * unscaled)

    along, squares = lax.fori_loop(0, NSEC, second, (zero, zero), unroll=2)
    along = jnp.sum(along, keepdims=True)
    squares = jnp.sum(squares, keepdims=True)
    rescale = 1.0 / jnp.sqrt((squares - along * along / weight) / float(NSEC * BS * BS) + 1e-06)
    share = along / weight

    def third(s, _):
        psi = vec[s].astype(jnp.float32)
        corr[s] = ((raw[s] - share * psi) * rescale).astype(jnp.bfloat16)
        return 0

    lax.fori_loop(0, NSEC, third, 0, unroll=2)
    corr_copy = pltpu.make_async_copy(corr.at[pl.ds(y * SECD, SECD)], corr_out, out_sem.at[1])
    corr_copy.start()

    apply(1, corr)
    sum_near(1)

    def spread_two(k, _):
        spot = two.at[c * HALF + k, mine]
        spot[...] = sum_far(1, k)
        for dx in FAR:
            for core in range(NC):
                send(spot, spot, x_send, x_recv.at[k], at(z, (x + dx) % NX, core, y))
        send(spot, spot, x_send, x_recv.at[k], sibling)
        return 0

    lax.fori_loop(0, HALF, spread_two, 0)
    for k in range(HALF):
        settle(inbox.at[1, 0, pl.ds(0, GROUP - 1)], x_recv.at[k])
    two_copy = pltpu.make_async_copy(two, two_out, out_sem.at[2])
    two_copy.start()

    for ref, ssem, fssem in ((vec, vsend, vfsend), (diag, dsend, dfsend)):
        settle(ref.at[pl.ds(0, 3 * HALF)], ssem)
        settle(ref.at[pl.ds(0, 3 * HALF)], fssem)
    for which in range(2):
        settle(inbox.at[which, :, pl.ds(0, GROUP - 1)], s1_send.at[which])
        settle(inbox.at[which, :, pl.ds(0, NZ - 1)], z_send.at[which])
    for k in range(HALF):
        settle(inbox.at[0, pl.ds(0, 3), pl.ds(0, NX * NY // 3)], xy_send.at[k])
    settle(vec.at[pl.ds(0, NY * HALF)], sib_send)
    settle(inbox.at[1, :, pl.ds(0, GROUP - 1)], x_send)
    one_copy.wait()
    corr_copy.wait()
    two_copy.wait()


def passed_on(a, b, c, a_out, b_out, c_out, sems):
    copies = [
        pltpu.make_async_copy(src, dst, sems.at[n])
        for n, (src, dst) in enumerate(((a, a_out), (b, b_out), (c, c_out)))
    ]
    for copy in copies:
        copy.start()
    for copy in copies:
        copy.wait()


def per_device(wavefunction, diagonal, left_ops, right_ops, connect):
    blocks = jax.ShapeDtypeStruct((SECD, BS, BS), jnp.bfloat16)
    dma = pltpu.SemaphoreType.DMA
    hbm = pl.BlockSpec(memory_space=pl.ANY)
    results = pl.pallas_call(
        kernel,
        out_shape=(blocks, blocks, blocks),
        in_specs=[hbm, hbm, hbm, hbm, pl.BlockSpec(memory_space=pltpu.SMEM)],
        out_specs=(hbm, hbm, hbm),
        scratch_shapes=[
            pltpu.VMEM((PAIRD, SECD, BS, BS), jnp.bfloat16),
            pltpu.VMEM((PAIRD, SECD, BS, BS), jnp.bfloat16),
            pltpu.VMEM((NSEC + 1, BS, BS), jnp.bfloat16),
            pltpu.VMEM((NSEC, BS, BS), jnp.float32),
            pltpu.VMEM((NY, SECD, BS, BS), jnp.bfloat16),
            pltpu.VMEM((NSEC, BS, BS), jnp.float32),
            pltpu.VMEM((NSEC + 1, BS, BS), jnp.bfloat16),
            pltpu.VMEM((2, SECD, BS, BS), jnp.bfloat16),
            pltpu.VMEM((2, HALF, GROUP, PIECE, BS), jnp.bfloat16),
            pltpu.VMEM((2, HALF, NZ, PIECE, BS), jnp.bfloat16),
            pltpu.VMEM((SECD, BS, BS), jnp.bfloat16),
            dma((2 * LOADS + 2,)), dma((3,)),
            dma, dma((6,)), dma, dma((NY,)), dma, dma((6,)), dma, dma((NY,)),
            dma((2,)), dma((2, HALF)), dma((2,)), dma((2, HALF)),
            dma((HALF,)), dma((HALF,)), dma, dma((HALF,)),
            dma, dma((HALF,)),
        ],
        compiler_params=pltpu.CompilerParams(
            collective_id=0, has_side_effects=True, vmem_limit_bytes=60 * 2**20
        ),
        name="davidson",
    )(wavefunction, diagonal, left_ops, right_ops, connect)
    return pl.pallas_call(
        passed_on,
        out_shape=(blocks, blocks, blocks),
        in_specs=[pl.BlockSpec(memory_space=pltpu.VMEM)] * 3,
        out_specs=(hbm, hbm, hbm),
        scratch_shapes=[dma((3,))],
        compiler_params=pltpu.CompilerParams(vmem_limit_bytes=60 * 2**20),
        name="passed_on",
    )(*results)


def solution(mesh):
    blocks = P("sec", None, None)
    ops = P("op", "sec", None, None)
    return jax.shard_map(
        per_device,
        mesh=mesh,
        in_specs=(blocks, blocks, ops, ops, P("op", "sec")),
        out_specs=(blocks, blocks, blocks),
        check_vma=False,
    )
```

```python
import functools

import jax
import jax.numpy as jnp
from jax import lax
from jax.experimental import pallas as pl
from jax.experimental.pallas import tpu as pltpu
from jax.sharding import PartitionSpec as P

MESH = pl.DeviceIdType.MESH
BS = 128
NZ, NX, NC, NY = 8, 4, 2, 4
GROUP = NX * NC
SECD = 10
HALF = SECD // NC
PIECE = BS // NX
NSEC = SECD * NY
PAIRD = 16
NT = (((1,), (1,)), ((), ()))
FAR_Z = (4, 3, 5, 2, 6, 1, 7)
FAR = (2, 1, 3)
LOADS = 4
UNROLL = 1


def reciprocal(q):
    guess = pl.reciprocal(q, approx=True)
    guess = guess * (2.0 - q * guess)
    return guess * (2.0 - q * guess)


def kernel(
    psi_hbm, diag_hbm, left_hbm, right_hbm, link,
    one_out, corr_out, two_out,
    left, right, vec, diag, sig, raw, corr, part, inbox, zbox, kept, two,
    load_sem, out_sem, vsend, vrecv, vfsend, vfrecv, dsend, drecv, dfsend, dfrecv,
    s1_send, s1_recv, z_send, z_recv, xy_send, xy_recv, sib_send, sib_recv,
    x_send, x_recv, own_sem,
):
    op = lax.axis_index("op")
    y = lax.axis_index("sec")
    z, x, c = op // (NX * NC), (op // NC) % NX, op % NC

    def at(z_, x_, c_, y_):
        return ((z_ * NX + x_) * NC + c_, y_)

    sibling = at(z, x, 1 - c, y)

    def send(src, dst, send_sem, recv_sem, device):
        pltpu.make_async_remote_copy(
            src_ref=src, dst_ref=dst, send_sem=send_sem, recv_sem=recv_sem, device_id=device, device_id_type=MESH
        ).start()

    def settle(ref, sem):
        pltpu.make_async_copy(ref, ref, sem).wait()

    per = PAIRD // LOADS
    loads = []
    for n in range(LOADS):
        rows = pl.ds(n * per, per)
        loads.append(pltpu.make_async_copy(left_hbm.at[rows], left.at[rows], load_sem.at[2 * n]))
        loads.append(pltpu.make_async_copy(right_hbm.at[rows], right.at[rows], load_sem.at[2 * n + 1]))
    own_vec = pltpu.make_async_copy(psi_hbm, vec.at[pl.ds(y * SECD, SECD)], load_sem.at[2 * LOADS])
    own_diag = pltpu.make_async_copy(diag_hbm, diag.at[pl.ds(y * SECD, SECD)], load_sem.at[2 * LOADS + 1])
    own_vec.start()
    for load in loads:
        load.start()
    own_diag.start()

    barrier = pltpu.get_barrier_semaphore()
    zs = [(z + dz) % NZ for dz in range(NZ)]
    xs = [(x + dx) % NX for dx in range(NX)]
    ys = [(y + dy) % NY for dy in range(NY)]
    along_z = [at(zs[dz], x, c, y) for dz in FAR_Z]
    along_x = [at(z, xs[dx], c, y) for dx in FAR]
    across_x = [at(z, xs[dx], 1 - c, y) for dx in FAR]
    along_xy = [at(z, xs[dx], c, ys[dy]) for dy in (2, 1, 3, 0) for dx in (2, 1, 3, 0) if dx or dy]
    friends = along_z + along_xy + across_x + [sibling]
    for friend in friends:
        pl.semaphore_signal(barrier, inc=1, device_id=friend, device_id_type=MESH)
    vec[NSEC] = jnp.zeros((BS, BS), jnp.bfloat16)
    raw[NSEC] = jnp.zeros((BS, BS), jnp.bfloat16)
    pl.semaphore_wait(barrier, len(friends))

    up, down = at(z, x, c, (y + 1) % NY), at(z, x, c, (y + NY - 1) % NY)

    def spot_of(ref, dy, core, rows):
        return ref.at[pl.ds(((y + dy) % NY) * SECD + core * HALF, HALF), rows]

    halves_of = (pl.ds(0, BS // 2), pl.ds(BS // 2, BS // 2))
    whole = pl.ds(0, BS)

    def gather_start(src, dst, ssem, rsem):
        for n, (there, h) in enumerate(((up, 0), (down, 1), (up, 1), (down, 0))):
            send(
                src.at[pl.ds(c * HALF, HALF), halves_of[h]], spot_of(dst, 0, c, halves_of[h]),
                ssem, rsem.at[n], there,
            )

    def gather_forward(dst, ssem, rsem):
        for dy, there, h, n in ((NY - 1, up, 0, 0), (1, down, 1, 1)):
            spot = spot_of(dst, dy, c, halves_of[h])
            settle(spot, rsem.at[n])
            send(spot, spot, ssem, rsem.at[4 + n], there)

    def gather_share(dst, rsem, fssem, frsem):
        for dy, n, rows in ((NY - 1, 2, whole), (1, 3, whole), (2, 4, halves_of[0]), (2, 5, halves_of[1])):
            settle(spot_of(dst, dy, c, halves_of[0]), rsem.at[n])
            spot = spot_of(dst, dy, c, rows)
            send(spot, spot, fssem, frsem.at[dy], sibling)

    def gather_end(dst, frsem):
        for dy in (NY - 1, 1, 2):
            settle(spot_of(dst, dy, 1 - c, whole), frsem.at[dy])

    gather_start(psi_hbm, vec, vsend, vrecv)
    own_vec.wait()
    gather_forward(vec, vsend, vrecv)
    gather_share(vec, vrecv, vfsend, vfrecv)
    gather_start(diag_hbm, diag, dsend, drecv)
    for load in loads:
        load.wait()
    gather_end(vec, vfrecv)

    mine = pl.ds(x * PIECE, PIECE)

    def apply(which, vector):
        def step(k, _):
            for core in (1 - c, c):
                b = core * HALF + k
                halves = []
                for p in range(PAIRD):
                    half = jnp.dot(left[p, b], vector[link[p, b]], preferred_element_type=jnp.float32)
                    halves.append(half.astype(jnp.bfloat16))
                halfway = jnp.concatenate(halves, axis=1)
                wide = jnp.concatenate([right[p, b] for p in range(PAIRD)], axis=1)
                total = lax.dot_general(halfway, wide, NT, preferred_element_type=jnp.float32)
                part[which, b] = total.astype(jnp.bfloat16)
                for dx, there in zip((2, 1, 3, 0), (along_x if core is c else across_x) + [sibling]):
                    rows = pl.ds(xs[dx] * PIECE, PIECE)
                    if core is c and dx == 0:
                        inbox[which, k, x * NC + c] = part[which, b, rows]
                    else:
                        send(
                            part.at[which, b, rows], inbox.at[which, k, x * NC + c],
                            s1_send.at[which], s1_recv.at[which, k], there,
                        )
            return 0

        lax.fori_loop(0, HALF, step, 0, unroll=UNROLL)

    def added(box, which, k, count):
        total = box[which, k, 0].astype(jnp.float32)
        for n in range(1, count):
            total = total + box[which, k, n].astype(jnp.float32)
        return total

    def sum_near(which):
        def step(k, _):
            settle(inbox.at[which, k, pl.ds(0, GROUP - 1)], s1_recv.at[which, k])
            zbox[which, k, z] = added(inbox, which, k, GROUP).astype(jnp.bfloat16)
            spot = zbox.at[which, k, z]
            for there in along_z:
                send(spot, spot, z_send.at[which], z_recv.at[which, k], there)
            return 0

        lax.fori_loop(0, HALF, step, 0)

    def sum_far(which, k):
        settle(zbox.at[which, k, pl.ds(0, NZ - 1)], z_recv.at[which, k])
        return added(zbox, which, k, NZ)

    apply(0, vec)
    gather_forward(diag, dsend, drecv)
    sum_near(0)

    def spread(k, _):
        spot = sig.at[y, c * HALF + k, mine]
        kept[k] = sum_far(0, k)
        spot[...] = kept[k].astype(jnp.bfloat16)
        for there in along_xy:
            send(spot, spot, xy_send.at[k], xy_recv.at[k], there)
        return 0

    lax.fori_loop(0, 2, spread, 0)
    gather_share(diag, drecv, dfsend, dfrecv)
    lax.fori_loop(2, HALF, spread, 0)

    def fold(block):
        return jnp.sum(block.reshape(BS // 8, 8, BS), axis=0)

    def first(core, k, sums):
        for g in range(NY):
            psi = vec[g * SECD + core * HALF + k].astype(jnp.float32)
            sigma = sig[g, core * HALF + k].astype(jnp.float32)
            sums = sums[0] + fold(psi * sigma), sums[1] + fold(psi * psi)
        return sums

    def hand(k, sums):
        settle(inbox.at[0, pl.ds(0, 3), pl.ds(0, NX * NY // 3)], xy_recv.at[k])
        spot = sig.at[:, c * HALF + k]
        send(spot, spot, sib_send, sib_recv.at[k], sibling)
        return first(c, k, sums)

    def handed(k, sums):
        settle(sig.at[:, (1 - c) * HALF + k], sib_recv.at[k])
        return first(1 - c, k, sums)

    zero = jnp.zeros((8, BS), jnp.float32)
    sums = lax.fori_loop(0, HALF, hand, (zero, zero))
    correlation, weight = lax.fori_loop(0, HALF, handed, sums)
    one_copy = pltpu.make_async_copy(sig.at[y], one_out, out_sem.at[0])
    one_copy.start()
    own_diag.wait()
    gather_end(diag, dfrecv)

    correlation = jnp.sum(correlation, keepdims=True)
    weight = jnp.sum(weight, keepdims=True)
    rayleigh = correlation / weight

    def unscaled_of(s):
        psi = vec[s].astype(jnp.float32)
        sigma = sig[s // SECD, s % SECD].astype(jnp.float32)
        shifted = diag[s] - rayleigh
        return psi, (sigma - rayleigh * psi) * shifted * reciprocal(shifted * shifted + 1.0)

    def second(s, sums):
        psi, unscaled = unscaled_of(s)
        raw[s] = unscaled.astype(jnp.bfloat16)
        return sums[0] + fold(psi * unscaled), sums[1] + fold(unscaled * unscaled)

    along, squares = lax.fori_loop(0, NSEC, second, (zero, zero), unroll=2)

    apply(1, raw)
    along = jnp.sum(along, keepdims=True)
    squares = jnp.sum(squares, keepdims=True)
    rescale = 1.0 / jnp.sqrt((squares - along * along / weight) / float(NSEC * BS * BS) + 1e-06)
    share = along / weight
    sum_near(1)

    def third(n, _):
        psi, unscaled = unscaled_of(y * SECD + n)
        corr[n] = ((unscaled - share * psi) * rescale).astype(jnp.bfloat16)
        return 0

    lax.fori_loop(0, SECD, third, 0, unroll=2)
    corr_copy = pltpu.make_async_copy(corr, corr_out, out_sem.at[1])
    corr_copy.start()

    def spread_two(k, _):
        spot, there = two.at[k], two_out.at[c * HALF + k, mine]
        spot[...] = ((sum_far(1, k) - share * kept[k]) * rescale).astype(jnp.bfloat16)
        for device in along_x + across_x + [sibling]:
            send(spot, there, x_send, x_recv.at[k], device)
        pltpu.make_async_copy(spot, there, own_sem).start()
        return 0

    lax.fori_loop(0, HALF, spread_two, 0)
    for k in range(HALF):
        settle(inbox.at[1, 0, pl.ds(0, GROUP - 1)], x_recv.at[k])

    for ref, ssem, fssem in ((vec, vsend, vfsend), (diag, dsend, dfsend)):
        settle(ref.at[pl.ds(0, 3 * HALF)], ssem)
        settle(ref.at[pl.ds(0, 3 * HALF)], fssem)
    for which in range(2):
        settle(inbox.at[which, :, pl.ds(0, GROUP - 1)], s1_send.at[which])
        settle(inbox.at[which, :, pl.ds(0, NZ - 1)], z_send.at[which])
    for k in range(HALF):
        settle(inbox.at[0, pl.ds(0, 3), pl.ds(0, NX * NY // 3)], xy_send.at[k])
    settle(vec.at[pl.ds(0, NY * HALF)], sib_send)
    settle(inbox.at[1, :, pl.ds(0, GROUP - 1)], x_send)
    one_copy.wait()
    corr_copy.wait()
    settle(two, own_sem)


def passed_on(a, b, c, a_out, b_out, c_out, held, sems):
    ins = [pltpu.make_async_copy(src, held.at[n], sems.at[0, n]) for n, src in enumerate((a, b, c))]
    outs = [pltpu.make_async_copy(held.at[n], dst, sems.at[1, n]) for n, dst in enumerate((a_out, b_out, c_out))]
    for copy in ins:
        copy.start()
    for copy, onward in zip(ins, outs):
        copy.wait()
        onward.start()
    for onward in outs:
        onward.wait()


def per_device(wavefunction, diagonal, left_ops, right_ops, connect):
    blocks = jax.ShapeDtypeStruct((SECD, BS, BS), jnp.bfloat16)
    dma = pltpu.SemaphoreType.DMA
    hbm = pl.BlockSpec(memory_space=pl.ANY)
    results = pl.pallas_call(
        kernel,
        out_shape=(blocks, blocks, blocks),
        in_specs=[hbm, hbm, hbm, hbm, pl.BlockSpec(memory_space=pltpu.SMEM)],
        out_specs=(hbm, hbm, hbm),
        scratch_shapes=[
            pltpu.VMEM((PAIRD, SECD, BS, BS), jnp.bfloat16),
            pltpu.VMEM((PAIRD, SECD, BS, BS), jnp.bfloat16),
            pltpu.VMEM((NSEC + 1, BS, BS), jnp.bfloat16),
            pltpu.VMEM((NSEC, BS, BS), jnp.float32),
            pltpu.VMEM((NY, SECD, BS, BS), jnp.bfloat16),
            pltpu.VMEM((NSEC + 1, BS, BS), jnp.bfloat16),
            pltpu.VMEM((SECD, BS, BS), jnp.bfloat16),
            pltpu.VMEM((2, SECD, BS, BS), jnp.bfloat16),
            pltpu.VMEM((2, HALF, GROUP, PIECE, BS), jnp.bfloat16),
            pltpu.VMEM((2, HALF, NZ, PIECE, BS), jnp.bfloat16),
            pltpu.VMEM((HALF, PIECE, BS), jnp.float32),
            pltpu.VMEM((HALF, PIECE, BS), jnp.bfloat16),
            dma((2 * LOADS + 2,)), dma((3,)),
            dma, dma((6,)), dma, dma((NY,)), dma, dma((6,)), dma, dma((NY,)),
            dma((2,)), dma((2, HALF)), dma((2,)), dma((2, HALF)),
            dma((HALF,)), dma((HALF,)), dma, dma((HALF,)),
            dma, dma((HALF,)), dma,
        ],
        compiler_params=pltpu.CompilerParams(
            collective_id=0, has_side_effects=True, vmem_limit_bytes=60 * 2**20
        ),
        name="davidson",
    )(wavefunction, diagonal, left_ops, right_ops, connect)
    return pl.pallas_call(
        passed_on,
        out_shape=(blocks, blocks, blocks),
        in_specs=[hbm, hbm, hbm],
        out_specs=(hbm, hbm, hbm),
        scratch_shapes=[pltpu.VMEM((3, SECD, BS, BS), jnp.bfloat16), dma((2, 3))],
        compiler_params=pltpu.CompilerParams(vmem_limit_bytes=60 * 2**20),
        name="passed_on",
    )(*results)


def solution(mesh):
    blocks = P("sec", None, None)
    ops = P("op", "sec", None, None)
    return jax.shard_map(
        per_device,
        mesh=mesh,
        in_specs=(blocks, blocks, ops, ops, P("op", "sec")),
        out_specs=(blocks, blocks, blocks),
        check_vma=False,
    )
```

```python
import functools

import jax
import jax.numpy as jnp
from jax import lax
from jax.experimental import pallas as pl
from jax.experimental.pallas import tpu as pltpu
from jax.sharding import PartitionSpec as P

MESH = pl.DeviceIdType.MESH
BS = 128
NZ, NX, NC, NY = 8, 4, 2, 4
GROUP = NX * NC
SECD = 10
HALF = SECD // NC
PIECE = BS // NX
NSEC = SECD * NY
PAIRD = 16
NT = (((1,), (1,)), ((), ()))
FAR_Z = (4, 3, 5, 2, 6, 1, 7)
FAR = (2, 1, 3)
LOADS = 4
UNROLL = 1
CUTS = 2


def reciprocal(q):
    guess = pl.reciprocal(q, approx=True)
    guess = guess * (2.0 - q * guess)
    return guess * (2.0 - q * guess)


def kernel(
    psi_hbm, diag_hbm, left_hbm, right_hbm, link,
    one_out, corr_out, two_out,
    left, right, vec, diag, sig, raw, corr, part, inbox, zbox, kept, two,
    load_sem, out_sem, vsend, vrecv, vfsend, vfrecv, dsend, drecv, dfsend, dfrecv,
    s1_send, s1_recv, z_send, z_recv, xy_send, xy_recv, sib_send, sib_recv,
    x_send, x_recv, own_sem,
):
    op = lax.axis_index("op")
    y = lax.axis_index("sec")
    z, x, c = op // (NX * NC), (op // NC) % NX, op % NC

    def at(z_, x_, c_, y_):
        return ((z_ * NX + x_) * NC + c_, y_)

    sibling = at(z, x, 1 - c, y)

    def send(src, dst, send_sem, recv_sem, device):
        pltpu.make_async_remote_copy(
            src_ref=src, dst_ref=dst, send_sem=send_sem, recv_sem=recv_sem, device_id=device, device_id_type=MESH
        ).start()

    def settle(ref, sem):
        pltpu.make_async_copy(ref, ref, sem).wait()

    barrier = pltpu.get_barrier_semaphore()
    zs = [(z + dz) % NZ for dz in range(NZ)]
    xs = [(x + dx) % NX for dx in range(NX)]
    ys = [(y + dy) % NY for dy in range(NY)]
    along_z = [at(zs[dz], x, c, y) for dz in FAR_Z]
    along_x = [at(z, xs[dx], c, y) for dx in FAR]
    across_x = [at(z, xs[dx], 1 - c, y) for dx in FAR]
    along_xy = [at(z, xs[dx], c, ys[dy]) for dy in (2, 1, 3, 0) for dx in (2, 1, 3, 0) if dx or dy]
    friends = [at(z, x, c, ys[dy]) for dy in FAR] + along_z + along_x + across_x + [sibling]
    friends += [at(z, xs[dx], c, ys[dy]) for dy in FAR for dx in FAR]
    for friend in friends:
        pl.semaphore_signal(barrier, inc=1, device_id=friend, device_id_type=MESH)
    per = PAIRD // LOADS
    loads = []
    for n in range(LOADS):
        rows = pl.ds(n * per, per)
        loads.append(pltpu.make_async_copy(left_hbm.at[rows], left.at[rows], load_sem.at[2 * n]))
        loads.append(pltpu.make_async_copy(right_hbm.at[rows], right.at[rows], load_sem.at[2 * n + 1]))
    own_vec = pltpu.make_async_copy(psi_hbm, vec.at[pl.ds(y * SECD, SECD)], load_sem.at[2 * LOADS])
    own_diag = pltpu.make_async_copy(diag_hbm, diag.at[pl.ds(y * SECD, SECD)], load_sem.at[2 * LOADS + 1])
    own_vec.start()
    for load in loads:
        load.start()
    own_diag.start()

    vec[NSEC] = jnp.zeros((BS, BS), jnp.bfloat16)
    raw[NSEC] = jnp.zeros((BS, BS), jnp.bfloat16)
    pl.semaphore_wait(barrier, len(friends))

    up, down = at(z, x, c, (y + 1) % NY), at(z, x, c, (y + NY - 1) % NY)

    def spot_of(ref, dy, core, rows):
        return ref.at[pl.ds(((y + dy) % NY) * SECD + core * HALF, HALF), rows]

    chunks = [pl.ds(q * (BS // CUTS), BS // CUTS) for q in range(CUTS)]
    whole = pl.ds(0, BS)
    early, late = range(CUTS // 2), range(CUTS // 2, CUTS)

    def gather_start(src, dst, ssem, rsem):
        for q in range(CUTS):
            for there, h, base in ((up, q, 0), (down, (q + CUTS // 2) % CUTS, CUTS)):
                send(
                    src.at[pl.ds(c * HALF, HALF), chunks[h]], spot_of(dst, 0, c, chunks[h]),
                    ssem, rsem.at[base + h], there,
                )

    def gather_forward(dst, ssem, rsem):
        for q in early:
            for dy, there, h, base in ((NY - 1, up, q, 0), (1, down, q + CUTS // 2, CUTS)):
                spot = spot_of(dst, dy, c, chunks[h])
                settle(spot, rsem.at[base + h])
                send(spot, spot, ssem, rsem.at[2 * CUTS + h], there)

    def gather_share(dst, rsem, fssem, frsem):
        def share(dy, h):
            spot = spot_of(dst, dy, c, chunks[h])
            send(spot, spot, fssem, frsem.at[dy], sibling)

        for q in early:
            share(NY - 1, q)
            share(1, q + CUTS // 2)
        for q in early:
            for dy, h, base in ((NY - 1, q + CUTS // 2, 0), (1, q, CUTS)):
                settle(spot_of(dst, dy, c, chunks[h]), rsem.at[base + h])
                share(dy, h)
        for q in early:
            for h in (q, q + CUTS // 2):
                settle(spot_of(dst, 2, c, chunks[h]), rsem.at[2 * CUTS + h])
                share(2, h)

    def gather_end(dst, frsem):
        for dy in (NY - 1, 1, 2):
            settle(spot_of(dst, dy, 1 - c, whole), frsem.at[dy])

    gather_start(psi_hbm, vec, vsend, vrecv)
    own_vec.wait()
    gather_forward(vec, vsend, vrecv)
    gather_share(vec, vrecv, vfsend, vfrecv)
    gather_start(diag_hbm, diag, dsend, drecv)
    for load in loads:
        load.wait()
    gather_end(vec, vfrecv)

    mine = pl.ds(x * PIECE, PIECE)

    def apply(which, vector):
        def step(k, _):
            for core in (c, 1 - c):
                b = core * HALF + k
                halves = []
                for p in range(PAIRD):
                    half = jnp.dot(left[p, b], vector[link[p, b]], preferred_element_type=jnp.float32)
                    halves.append(half.astype(jnp.bfloat16))
                halfway = jnp.concatenate(halves, axis=1)
                wide = jnp.concatenate([right[p, b] for p in range(PAIRD)], axis=1)
                total = lax.dot_general(halfway, wide, NT, preferred_element_type=jnp.float32)
                part[which, b] = total.astype(jnp.bfloat16)
                for dx, there in zip((2, 1, 3, 0), (along_x if core is c else across_x) + [sibling]):
                    rows = pl.ds(xs[dx] * PIECE, PIECE)
                    if core is c and dx == 0:
                        inbox[which, k, x * NC + c] = part[which, b, rows]
                    else:
                        send(
                            part.at[which, b, rows], inbox.at[which, k, x * NC + c],
                            s1_send.at[which], s1_recv.at[which, k], there,
                        )
            return 0

        for lo, hi, near in ((0, 4, 0), (4, 5, 1)):
            lax.fori_loop(lo, hi, step, 0)
            if near:
                sum_near(which, 0, near)

    def added(box, which, k, count):
        total = box[which, k, 0].astype(jnp.float32)
        for n in range(1, count):
            total = total + box[which, k, n].astype(jnp.float32)
        return total

    def sum_near(which, lo=0, hi=HALF):
        def step(k, _):
            settle(inbox.at[which, k, pl.ds(0, GROUP - 1)], s1_recv.at[which, k])
            zbox[which, k, z] = added(inbox, which, k, GROUP).astype(jnp.bfloat16)
            spot = zbox.at[which, k, z]
            for there in along_z:
                send(spot, spot, z_send.at[which], z_recv.at[which, k], there)
            return 0

        lax.fori_loop(lo, hi, step, 0, unroll=hi - lo)

    def sum_far(which, k):
        settle(zbox.at[which, k, pl.ds(0, NZ - 1)], z_recv.at[which, k])
        return added(zbox, which, k, NZ)

    apply(0, vec)
    gather_forward(diag, dsend, drecv)
    sum_near(0, 1)

    def spread(k, _):
        spot = sig.at[y, c * HALF + k, mine]
        kept[k] = sum_far(0, k)
        spot[...] = kept[k].astype(jnp.bfloat16)
        for there in along_xy:
            send(spot, spot, xy_send.at[k], xy_recv.at[k], there)
        return 0

    lax.fori_loop(0, 2, spread, 0, unroll=2)
    gather_share(diag, drecv, dfsend, dfrecv)
    lax.fori_loop(2, HALF, spread, 0, unroll=HALF - 2)

    def fold(block):
        return jnp.sum(block.reshape(BS // 8, 8, BS), axis=0)

    def first(core, k, sums):
        for g in range(NY):
            psi = vec[g * SECD + core * HALF + k].astype(jnp.float32)
            sigma = sig[g, core * HALF + k].astype(jnp.float32)
            sums = sums[0] + fold(psi * sigma), sums[1] + fold(psi * psi)
        return sums

    def hand(k, sums):
        settle(inbox.at[0, pl.ds(0, 3), pl.ds(0, NX * NY // 3)], xy_recv.at[k])
        spot = sig.at[:, c * HALF + k]
        send(spot, spot, sib_send, sib_recv.at[k], sibling)
        return first(c, k, sums)

    def handed(k, sums):
        settle(sig.at[:, (1 - c) * HALF + k], sib_recv.at[k])
        return first(1 - c, k, sums)

    zero = jnp.zeros((8, BS), jnp.float32)
    sums = lax.fori_loop(0, HALF, hand, (zero, zero), unroll=HALF)
    correlation, weight = lax.fori_loop(0, HALF, handed, sums, unroll=HALF)
    one_copy = pltpu.make_async_copy(sig.at[y], one_out, out_sem.at[0])
    one_copy.start()
    own_diag.wait()
    gather_end(diag, dfrecv)

    correlation = jnp.sum(correlation, keepdims=True)
    weight = jnp.sum(weight, keepdims=True)
    rayleigh = correlation / weight

    def unscaled_of(s):
        psi = vec[s].astype(jnp.float32)
        sigma = sig[s // SECD, s % SECD].astype(jnp.float32)
        shifted = diag[s] - rayleigh
        return psi, (sigma - rayleigh * psi) * shifted * reciprocal(shifted * shifted + 1.0)

    def second(s, sums):
        psi, unscaled = unscaled_of(s)
        raw[s] = unscaled.astype(jnp.bfloat16)
        return sums[0] + fold(psi * unscaled), sums[1] + fold(unscaled * unscaled)

    along, squares = lax.fori_loop(0, NSEC, second, (zero, zero), unroll=4)

    apply(1, raw)
    along = jnp.sum(along, keepdims=True)
    squares = jnp.sum(squares, keepdims=True)
    rescale = 1.0 / jnp.sqrt((squares - along * along / weight) / float(NSEC * BS * BS) + 1e-06)
    share = along / weight
    sum_near(1, 1)

    def third(n, _):
        psi, unscaled = unscaled_of(y * SECD + n)
        corr[n] = ((unscaled - share * psi) * rescale).astype(jnp.bfloat16)
        return 0

    lax.fori_loop(0, SECD, third, 0, unroll=2)
    corr_copy = pltpu.make_async_copy(corr, corr_out, out_sem.at[1])
    corr_copy.start()

    def spread_two(k, _):
        spot, there = two.at[k], two_out.at[c * HALF + k, mine]
        spot[...] = ((sum_far(1, k) - share * kept[k]) * rescale).astype(jnp.bfloat16)
        for device in along_x + across_x + [sibling]:
            send(spot, there, x_send, x_recv.at[k], device)
        pltpu.make_async_copy(spot, there, own_sem).start()
        return 0

    lax.fori_loop(0, HALF, spread_two, 0, unroll=HALF)
    for k in range(HALF):
        settle(inbox.at[1, 0, pl.ds(0, GROUP - 1)], x_recv.at[k])

    for ref, ssem, fssem in ((vec, vsend, vfsend), (diag, dsend, dfsend)):
        settle(ref.at[pl.ds(0, 3 * HALF)], ssem)
        settle(ref.at[pl.ds(0, 3 * HALF)], fssem)
    for which in range(2):
        settle(inbox.at[which, :, pl.ds(0, GROUP - 1)], s1_send.at[which])
        settle(inbox.at[which, :, pl.ds(0, NZ - 1)], z_send.at[which])
    for k in range(HALF):
        settle(inbox.at[0, pl.ds(0, 3), pl.ds(0, NX * NY // 3)], xy_send.at[k])
    settle(vec.at[pl.ds(0, NY * HALF)], sib_send)
    settle(inbox.at[1, :, pl.ds(0, GROUP - 1)], x_send)
    one_copy.wait()
    corr_copy.wait()
    settle(two, own_sem)


def passed_on(a, b, c, a_out, b_out, c_out, held, sems):
    ins = [pltpu.make_async_copy(src, held.at[n], sems.at[0, n]) for n, src in enumerate((a, b, c))]
    outs = [pltpu.make_async_copy(held.at[n], dst, sems.at[1, n]) for n, dst in enumerate((a_out, b_out, c_out))]
    for copy in ins:
        copy.start()
    for copy, onward in zip(ins, outs):
        copy.wait()
        onward.start()
    for onward in outs:
        onward.wait()


def per_device(wavefunction, diagonal, left_ops, right_ops, connect):
    blocks = jax.ShapeDtypeStruct((SECD, BS, BS), jnp.bfloat16)
    dma = pltpu.SemaphoreType.DMA
    hbm = pl.BlockSpec(memory_space=pl.ANY)
    results = pl.pallas_call(
        kernel,
        out_shape=(blocks, blocks, blocks),
        in_specs=[hbm, hbm, hbm, hbm, pl.BlockSpec(memory_space=pltpu.SMEM)],
        out_specs=(hbm, hbm, hbm),
        scratch_shapes=[
            pltpu.VMEM((PAIRD, SECD, BS, BS), jnp.bfloat16),
            pltpu.VMEM((PAIRD, SECD, BS, BS), jnp.bfloat16),
            pltpu.VMEM((NSEC + 1, BS, BS), jnp.bfloat16),
            pltpu.VMEM((NSEC, BS, BS), jnp.float32),
            pltpu.VMEM((NY, SECD, BS, BS), jnp.bfloat16),
            pltpu.VMEM((NSEC + 1, BS, BS), jnp.bfloat16),
            pltpu.VMEM((SECD, BS, BS), jnp.bfloat16),
            pltpu.VMEM((2, SECD, BS, BS), jnp.bfloat16),
            pltpu.VMEM((2, HALF, GROUP, PIECE, BS), jnp.bfloat16),
            pltpu.VMEM((2, HALF, NZ, PIECE, BS), jnp.bfloat16),
            pltpu.VMEM((HALF, PIECE, BS), jnp.float32),
            pltpu.VMEM((HALF, PIECE, BS), jnp.bfloat16),
            dma((2 * LOADS + 2,)), dma((3,)),
            dma, dma((3 * CUTS,)), dma, dma((NY,)), dma, dma((3 * CUTS,)), dma, dma((NY,)),
            dma((2,)), dma((2, HALF)), dma((2,)), dma((2, HALF)),
            dma((HALF,)), dma((HALF,)), dma, dma((HALF,)),
            dma, dma((HALF,)), dma,
        ],
        compiler_params=pltpu.CompilerParams(
            collective_id=0, has_side_effects=True, vmem_limit_bytes=60 * 2**20
        ),
        name="davidson",
    )(wavefunction, diagonal, left_ops, right_ops, connect)
    return pl.pallas_call(
        passed_on,
        out_shape=(blocks, blocks, blocks),
        in_specs=[hbm, hbm, hbm],
        out_specs=(hbm, hbm, hbm),
        scratch_shapes=[pltpu.VMEM((3, SECD, BS, BS), jnp.bfloat16), dma((2, 3))],
        compiler_params=pltpu.CompilerParams(vmem_limit_bytes=60 * 2**20),
        name="passed_on",
    )(*results)


def solution(mesh):
    blocks = P("sec", None, None)
    ops = P("op", "sec", None, None)
    return jax.shard_map(
        per_device,
        mesh=mesh,
        in_specs=(blocks, blocks, ops, ops, P("op", "sec")),
        out_specs=(blocks, blocks, blocks),
        check_vma=False,
    )
```

```python
import functools

import jax
import jax.numpy as jnp
from jax import lax
from jax.experimental import pallas as pl
from jax.experimental.pallas import tpu as pltpu
from jax.sharding import PartitionSpec as P

MESH = pl.DeviceIdType.MESH
BS = 128
NZ, NX, NC, NY = 8, 4, 2, 4
GROUP = NX * NC
SECD = 10
HALF = SECD // NC
PIECE = BS // NX
NSEC = SECD * NY
PAIRD = 16
NT = (((1,), (1,)), ((), ()))
FAR_Z = (4, 3, 5, 2, 6, 1, 7)
FAR = (2, 1, 3)
LOADS = 4
UNROLL = 1
CUTS = 2


def reciprocal(q):
    guess = pl.reciprocal(q, approx=True)
    guess = guess * (2.0 - q * guess)
    return guess * (2.0 - q * guess)


def kernel(
    psi_hbm, diag_hbm, left_hbm, right_hbm, link,
    one_out, corr_out, two_out,
    left, right, vec, diag, sig, raw, corr, part, inbox, zbox, kept, two,
    load_sem, out_sem, vsend, vrecv, vfsend, vfrecv, dsend, drecv, dfsend, dfrecv,
    s1_send, s1_recv, z_send, z_recv, xy_send, xy_recv, sib_send, sib_recv,
    x_send, x_recv, own_sem,
):
    op = lax.axis_index("op")
    y = lax.axis_index("sec")
    z, x, c = op // (NX * NC), (op // NC) % NX, op % NC

    def at(z_, x_, c_, y_):
        return ((z_ * NX + x_) * NC + c_, y_)

    sibling = at(z, x, 1 - c, y)

    def send(src, dst, send_sem, recv_sem, device):
        pltpu.make_async_remote_copy(
            src_ref=src, dst_ref=dst, send_sem=send_sem, recv_sem=recv_sem, device_id=device, device_id_type=MESH
        ).start()

    def settle(ref, sem):
        pltpu.make_async_copy(ref, ref, sem).wait()

    barrier = pltpu.get_barrier_semaphore()
    zs = [(z + dz) % NZ for dz in range(NZ)]
    xs = [(x + dx) % NX for dx in range(NX)]
    ys = [(y + dy) % NY for dy in range(NY)]
    along_z = [at(zs[dz], x, c, y) for dz in FAR_Z]
    along_x = [at(z, xs[dx], c, y) for dx in FAR]
    across_x = [at(z, xs[dx], 1 - c, y) for dx in FAR]
    along_xy = [at(z, xs[dx], c, ys[dy]) for dy in (2, 1, 3, 0) for dx in (2, 1, 3, 0) if dx or dy]
    friends = [at(z, x, c, ys[dy]) for dy in FAR] + along_z + along_x + across_x + [sibling]
    friends += [at(z, xs[dx], c, ys[dy]) for dy in FAR for dx in FAR]
    for friend in friends:
        pl.semaphore_signal(barrier, inc=1, device_id=friend, device_id_type=MESH)
    per = PAIRD // LOADS
    loads = []
    for n in range(LOADS):
        rows = pl.ds(n * per, per)
        loads.append(pltpu.make_async_copy(left_hbm.at[rows], left.at[rows], load_sem.at[2 * n]))
        loads.append(pltpu.make_async_copy(right_hbm.at[rows], right.at[rows], load_sem.at[2 * n + 1]))
    own_vec = pltpu.make_async_copy(psi_hbm, vec.at[pl.ds(y * SECD, SECD)], load_sem.at[2 * LOADS])
    own_diag = pltpu.make_async_copy(diag_hbm, diag.at[pl.ds(y * SECD, SECD)], load_sem.at[2 * LOADS + 1])
    own_vec.start()
    for load in loads:
        load.start()
    own_diag.start()

    vec[NSEC] = jnp.zeros((BS, BS), jnp.bfloat16)
    raw[NSEC] = jnp.zeros((BS, BS), jnp.bfloat16)
    pl.semaphore_wait(barrier, len(friends))

    up, down = at(z, x, c, (y + 1) % NY), at(z, x, c, (y + NY - 1) % NY)

    def spot_of(ref, dy, core, rows):
        return ref.at[pl.ds(((y + dy) % NY) * SECD + core * HALF, HALF), rows]

    chunks = [pl.ds(q * (BS // CUTS), BS // CUTS) for q in range(CUTS)]
    whole = pl.ds(0, BS)
    early, late = range(CUTS // 2), range(CUTS // 2, CUTS)

    def gather_start(src, dst, ssem, rsem):
        for q in range(CUTS):
            for there, h, base in ((up, q, 0), (down, (q + CUTS // 2) % CUTS, CUTS)):
                send(
                    src.at[pl.ds(c * HALF, HALF), chunks[h]], spot_of(dst, 0, c, chunks[h]),
                    ssem, rsem.at[base + h], there,
                )

    def gather_forward(dst, ssem, rsem):
        for q in early:
            for dy, there, h, base in ((NY - 1, up, q, 0), (1, down, q + CUTS // 2, CUTS)):
                spot = spot_of(dst, dy, c, chunks[h])
                settle(spot, rsem.at[base + h])
                send(spot, spot, ssem, rsem.at[2 * CUTS + h], there)

    def gather_share(dst, rsem, fssem, frsem):
        def share(dy, h):
            spot = spot_of(dst, dy, c, chunks[h])
            send(spot, spot, fssem, frsem.at[dy], sibling)

        for q in early:
            share(NY - 1, q)
            share(1, q + CUTS // 2)
        for q in early:
            for dy, h, base in ((NY - 1, q + CUTS // 2, 0), (1, q, CUTS)):
                settle(spot_of(dst, dy, c, chunks[h]), rsem.at[base + h])
                share(dy, h)
        for q in early:
            for h in (q, q + CUTS // 2):
                settle(spot_of(dst, 2, c, chunks[h]), rsem.at[2 * CUTS + h])
                share(2, h)

    def gather_end(dst, frsem):
        for dy in (NY - 1, 1, 2):
            settle(spot_of(dst, dy, 1 - c, whole), frsem.at[dy])

    gather_start(psi_hbm, vec, vsend, vrecv)
    own_vec.wait()
    gather_forward(vec, vsend, vrecv)
    gather_share(vec, vrecv, vfsend, vfrecv)
    gather_start(diag_hbm, diag, dsend, drecv)
    for load in loads:
        load.wait()
    gather_end(vec, vfrecv)

    mine = pl.ds(x * PIECE, PIECE)

    def apply(which, vector):
        def step(k, _):
            for core in (c, 1 - c):
                b = core * HALF + k
                halves = []
                for p in range(PAIRD):
                    half = jnp.dot(left[p, b], vector[link[p, b]], preferred_element_type=jnp.float32)
                    halves.append(half.astype(jnp.bfloat16))
                halfway = jnp.concatenate(halves, axis=1)
                wide = jnp.concatenate([right[p, b] for p in range(PAIRD)], axis=1)
                total = lax.dot_general(halfway, wide, NT, preferred_element_type=jnp.float32)
                part[which, b] = total.astype(jnp.bfloat16)
                for dx, there in zip((2, 1, 3, 0), (along_x if core is c else across_x) + [sibling]):
                    rows = pl.ds(xs[dx] * PIECE, PIECE)
                    if core is c and dx == 0:
                        inbox[which, k, x * NC + c] = part[which, b, rows]
                    else:
                        send(
                            part.at[which, b, rows], inbox.at[which, k, x * NC + c],
                            s1_send.at[which], s1_recv.at[which, k], there,
                        )
            return 0

        for lo, hi, near in ((0, 4, 0), (4, 5, 1)):
            lax.fori_loop(lo, hi, step, 0)
            if near:
                sum_near(which, 0, near)

    def added(box, which, k, count):
        total = box[which, k, 0].astype(jnp.float32)
        for n in range(1, count):
            total = total + box[which, k, n].astype(jnp.float32)
        return total

    def sum_near(which, lo=0, hi=HALF):
        def step(k, _):
            settle(inbox.at[which, k, pl.ds(0, GROUP - 1)], s1_recv.at[which, k])
            zbox[which, k, z] = added(inbox, which, k, GROUP).astype(jnp.bfloat16)
            spot = zbox.at[which, k, z]
            for there in along_z:
                send(spot, spot, z_send.at[which], z_recv.at[which, k], there)
            return 0

        lax.fori_loop(lo, hi, step, 0, unroll=hi - lo)

    def sum_far(which, k):
        settle(zbox.at[which, k, pl.ds(0, NZ - 1)], z_recv.at[which, k])
        return added(zbox, which, k, NZ)

    apply(0, vec)
    gather_forward(diag, dsend, drecv)
    sum_near(0, 1)

    def spread(k, _):
        spot = sig.at[y, c * HALF + k, mine]
        kept[k] = sum_far(0, k)
        spot[...] = kept[k].astype(jnp.bfloat16)
        for there in along_xy:
            send(spot, spot, xy_send.at[k], xy_recv.at[k], there)
        return 0

    lax.fori_loop(0, 2, spread, 0, unroll=2)
    gather_share(diag, drecv, dfsend, dfrecv)
    lax.fori_loop(2, HALF, spread, 0, unroll=HALF - 2)

    def fold(block):
        return jnp.sum(block.reshape(BS // 8, 8, BS), axis=0)

    def first(core, k, sums):
        for g in range(NY):
            psi = vec[g * SECD + core * HALF + k].astype(jnp.float32)
            sigma = sig[g, core * HALF + k].astype(jnp.float32)
            sums = sums[0] + fold(psi * sigma), sums[1] + fold(psi * psi)
        return sums

    def hand(k, sums):
        settle(inbox.at[0, pl.ds(0, 3), pl.ds(0, NX * NY // 3)], xy_recv.at[k])
        spot = sig.at[:, c * HALF + k]
        send(spot, spot, sib_send, sib_recv.at[k], sibling)
        return first(c, k, sums)

    def handed(k, sums):
        settle(sig.at[:, (1 - c) * HALF + k], sib_recv.at[k])
        return first(1 - c, k, sums)

    zero = jnp.zeros((8, BS), jnp.float32)
    sums = lax.fori_loop(0, HALF, hand, (zero, zero), unroll=HALF)
    correlation, weight = lax.fori_loop(0, HALF, handed, sums, unroll=HALF)
    one_copy = pltpu.make_async_copy(sig.at[y], one_out, out_sem.at[0])
    one_copy.start()
    own_diag.wait()
    gather_end(diag, dfrecv)

    correlation = jnp.sum(correlation, keepdims=True)
    weight = jnp.sum(weight, keepdims=True)
    rayleigh = correlation / weight

    def unscaled_of(s):
        psi = vec[s].astype(jnp.float32)
        sigma = sig[s // SECD, s % SECD].astype(jnp.float32)
        shifted = diag[s] - rayleigh
        return psi, (sigma - rayleigh * psi) * shifted * reciprocal(shifted * shifted + 1.0)

    def second(s, sums):
        psi, unscaled = unscaled_of(s)
        raw[s] = unscaled.astype(jnp.bfloat16)
        return sums[0] + fold(psi * unscaled), sums[1] + fold(unscaled * unscaled)

    along, squares = lax.fori_loop(0, NSEC, second, (zero, zero), unroll=4)

    apply(1, raw)
    along = jnp.sum(along, keepdims=True)
    squares = jnp.sum(squares, keepdims=True)
    rescale = 1.0 / jnp.sqrt((squares - along * along / weight) / float(NSEC * BS * BS) + 1e-06)
    share = along / weight
    sum_near(1, 1)

    def third(n, _):
        psi, unscaled = unscaled_of(y * SECD + n)
        corr[n] = ((unscaled - share * psi) * rescale).astype(jnp.bfloat16)
        return 0

    lax.fori_loop(0, SECD, third, 0, unroll=2)
    corr_copy = pltpu.make_async_copy(corr, corr_out, out_sem.at[1])
    corr_copy.start()

    def spread_two(k, _):
        spot, there = two.at[k], two_out.at[c * HALF + k, mine]
        spot[...] = ((sum_far(1, k) - share * kept[k]) * rescale).astype(jnp.bfloat16)
        for device in [across_x[0], along_x[0]] + across_x[1:] + along_x[1:] + [sibling]:
            send(spot, there, x_send, x_recv.at[k], device)
        pltpu.make_async_copy(spot, there, own_sem).start()
        return 0

    lax.fori_loop(0, HALF, spread_two, 0, unroll=HALF)
    for k in range(HALF):
        settle(inbox.at[1, 0, pl.ds(0, GROUP - 1)], x_recv.at[k])

    for ref, ssem, fssem in ((vec, vsend, vfsend), (diag, dsend, dfsend)):
        settle(ref.at[pl.ds(0, 3 * HALF)], ssem)
        settle(ref.at[pl.ds(0, 3 * HALF)], fssem)
    for which in range(2):
        settle(inbox.at[which, :, pl.ds(0, GROUP - 1)], s1_send.at[which])
        settle(inbox.at[which, :, pl.ds(0, NZ - 1)], z_send.at[which])
    for k in range(HALF):
        settle(inbox.at[0, pl.ds(0, 3), pl.ds(0, NX * NY // 3)], xy_send.at[k])
    settle(vec.at[pl.ds(0, NY * HALF)], sib_send)
    settle(inbox.at[1, :, pl.ds(0, GROUP - 1)], x_send)
    one_copy.wait()
    corr_copy.wait()
    settle(two, own_sem)


def passed_on(a, b, c, a_out, b_out, c_out, held, sems):
    ins, outs = [], []
    for n, (src, dst) in enumerate(((a, a_out), (b, b_out), (c, c_out))):
        for h in range(2):
            rows = pl.ds(h * HALF, HALF)
            ins.append(pltpu.make_async_copy(src.at[rows], held.at[n, rows], sems.at[0, 2 * n + h]))
            outs.append(pltpu.make_async_copy(held.at[n, rows], dst.at[rows], sems.at[1, 2 * n + h]))
    for copy in ins:
        copy.start()
    for copy, onward in zip(ins, outs):
        copy.wait()
        onward.start()
    for onward in outs:
        onward.wait()


def per_device(wavefunction, diagonal, left_ops, right_ops, connect):
    blocks = jax.ShapeDtypeStruct((SECD, BS, BS), jnp.bfloat16)
    dma = pltpu.SemaphoreType.DMA
    hbm = pl.BlockSpec(memory_space=pl.ANY)
    results = pl.pallas_call(
        kernel,
        out_shape=(blocks, blocks, blocks),
        in_specs=[hbm, hbm, hbm, hbm, pl.BlockSpec(memory_space=pltpu.SMEM)],
        out_specs=(hbm, hbm, hbm),
        scratch_shapes=[
            pltpu.VMEM((PAIRD, SECD, BS, BS), jnp.bfloat16),
            pltpu.VMEM((PAIRD, SECD, BS, BS), jnp.bfloat16),
            pltpu.VMEM((NSEC + 1, BS, BS), jnp.bfloat16),
            pltpu.VMEM((NSEC, BS, BS), jnp.float32),
            pltpu.VMEM((NY, SECD, BS, BS), jnp.bfloat16),
            pltpu.VMEM((NSEC + 1, BS, BS), jnp.bfloat16),
            pltpu.VMEM((SECD, BS, BS), jnp.bfloat16),
            pltpu.VMEM((2, SECD, BS, BS), jnp.bfloat16),
            pltpu.VMEM((2, HALF, GROUP, PIECE, BS), jnp.bfloat16),
            pltpu.VMEM((2, HALF, NZ, PIECE, BS), jnp.bfloat16),
            pltpu.VMEM((HALF, PIECE, BS), jnp.float32),
            pltpu.VMEM((HALF, PIECE, BS), jnp.bfloat16),
            dma((2 * LOADS + 2,)), dma((3,)),
            dma, dma((3 * CUTS,)), dma, dma((NY,)), dma, dma((3 * CUTS,)), dma, dma((NY,)),
            dma((2,)), dma((2, HALF)), dma((2,)), dma((2, HALF)),
            dma((HALF,)), dma((HALF,)), dma, dma((HALF,)),
            dma, dma((HALF,)), dma,
        ],
        compiler_params=pltpu.CompilerParams(
            collective_id=0, has_side_effects=True, vmem_limit_bytes=60 * 2**20
        ),
        name="davidson",
    )(wavefunction, diagonal, left_ops, right_ops, connect)
    return pl.pallas_call(
        passed_on,
        out_shape=(blocks, blocks, blocks),
        in_specs=[hbm, hbm, hbm],
        out_specs=(hbm, hbm, hbm),
        scratch_shapes=[pltpu.VMEM((3, SECD, BS, BS), jnp.bfloat16), dma((2, 6))],
        compiler_params=pltpu.CompilerParams(vmem_limit_bytes=60 * 2**20),
        name="passed_on",
    )(*results)


def solution(mesh):
    blocks = P("sec", None, None)
    ops = P("op", "sec", None, None)
    return jax.shard_map(
        per_device,
        mesh=mesh,
        in_specs=(blocks, blocks, ops, ops, P("op", "sec")),
        out_specs=(blocks, blocks, blocks),
        check_vma=False,
    )
```
